32 devices in a mesh: row: 4 (over y, core), col: 8 (over z, x).
Axes of the slice: x: 2, y: 2, z: 4, core: 2. Of those that a mesh axis runs over, the one named last changes fastest.
Arguments:
- layer_input: bfloat16 [1024, 12288], P('col', 'row'), may hold values from -6 to 6
- out_grad: bfloat16 [1024, 12288], P('col', 'row'), may hold values from -6 to 6
- preact: bfloat16 [1024, 16384], P('row', 'col'), may hold values from -6 to 6
- weight_in: bfloat16 [12288, 16384], P('row', 'col'), may hold values from -0.0546875 to 0.0546875
- weight_out: bfloat16 [16384, 12288], P('col', 'row'), may hold values from -0.046875 to 0.046875
Outputs:
- input_grad: bfloat16 [1024, 12288], P('col', 'row')
- weight_in_grad: float32 [12288, 16384], P('row', 'col')
- weight_out_grad: float32 [16384, 12288], P('col', 'row')
The draws below stay inside these ranges and needn't reach their ends.
All inputs are finite; a program needn't handle non-finite values.
Results may differ from the reference program's by a relative error of at most 0.019.
Values may be sent and summed in bfloat16 or wider, within the bound.
A program may use at most 192 MiB of HBM per device.

```python
import math
import jax
import jax.numpy as jnp

D = 12288
FF = 16384
TOKENS = 1024


def spiked(entries, rng, source, target, parts, factor):
    def block_of(position):
        return (jnp.arange(entries.shape[position]) // (entries.shape[position] // parts)).reshape((-1,) + (1,) * (entries.ndim - 1 - position))

    first = jax.random.permutation(rng, parts)[block_of(target)]
    other_side = (block_of(target) + parts // 2) % parts
    return jnp.where((block_of(source) == first) | (block_of(source) == other_side), factor * entries, entries)


def level_of(key, extent, shards, smallest, high):
    def one(position, blocks):
        steps = jax.random.uniform(jax.random.fold_in(jax.random.fold_in(key, 6), position), (blocks,), jnp.float32, smallest / len(shards), high / len(shards))
        return jnp.repeat(jnp.exp(steps), extent[position] // blocks).reshape((-1,) + (1,) * (len(extent) - position - 1))

    factor_of = one(*shards[0])
    for cut in shards[1:]:
        factor_of = factor_of * one(*cut)
    return factor_of


def noise(key, extent, spread, bound, pieces=(), kind=jnp.bfloat16):
    factor_of = level_of(key, extent, pieces, -0.22, 0.18) if pieces else 1.0
    entries = jax.random.normal(key, extent, jnp.float32) * spread * factor_of
    return jnp.minimum(jnp.maximum(entries, -bound), bound).astype(kind)


def bell_draw_with(own_key, extent, deviation, bound, shards, heavy, held_as=jnp.bfloat16):
    entries = deviation * jax.random.normal(own_key, extent, jnp.float32)
    if shards:
        entries = entries * level_of(own_key, extent, shards, -0.22, 0.18)
    return jnp.clip(spiked(entries, jax.random.fold_in(own_key, 3), *heavy), -bound, bound).astype(held_as)


def setup_inputs(seed: int = 0) -> dict:
    splits = jax.random.split(jax.random.key(seed), 6)
    layer_input = noise(splits[0], (TOKENS, D), 1.0, 6.0, ((0, 8), (1, 4)))
    out_grad = bell_draw_with(splits[1], (TOKENS, D), 1.0, 6.0, ((0, 8), (1, 4)), (1, 0, 8, 2.0))
    preact = noise(splits[2], (TOKENS, FF), 1.5, 6.0, ((0, 4), (1, 8)))
    weight_in = noise(splits[3], (D, FF), D ** -0.5, 0.0546875, ((0, 4), (1, 8)))
    weight_out = noise(splits[4], (FF, D), FF ** -0.5, 0.046875, ((0, 8), (1, 4)))
    return {"layer_input": layer_input, "out_grad": out_grad, "preact": preact, "weight_in": weight_in, "weight_out": weight_out}


def gelu_parts(h):
    c = math.sqrt(2.0 / math.pi)
    t = jnp.tanh(c * (h + 0.044715 * h * h * h))
    value = 0.5 * h * (1.0 + t)
    slope = 0.5 * (1.0 + t) + 0.5 * h * (1.0 - t * t) * c * (1.0 + 3.0 * 0.044715 * h * h)
    return (value, slope)

def reference(layer_input, out_grad, preact, weight_in, weight_out):
    hidden = preact.astype(jnp.float32)
    value, slope = gelu_parts(hidden)
    activ = value.astype(jnp.bfloat16)
    grad_act = jnp.dot(out_grad, weight_out.T, preferred_element_type=jnp.float32)
    grad_pre = (grad_act * slope).astype(jnp.bfloat16)
    weight_out_grad = jnp.dot(activ.T, out_grad, preferred_element_type=jnp.float32)
    weight_in_grad = jnp.dot(layer_input.T, grad_pre, preferred_element_type=jnp.float32)
    input_grad = jnp.dot(grad_pre, weight_in.T, preferred_element_type=jnp.float32).astype(jnp.bfloat16)
    return (input_grad, weight_in_grad, weight_out_grad)
```

```python
import functools
import math

import jax
import jax.numpy as jnp
from jax import lax
from jax.experimental import pallas as pl
from jax.experimental.pallas import tpu as pltpu
from jax.sharding import PartitionSpec as P

MESH = pl.DeviceIdType.MESH
BF16 = jnp.bfloat16
F32 = jnp.float32


def gelu_parts(h):
    c = math.sqrt(2.0 / math.pi)
    t = jnp.tanh(c * (h + 0.044715 * h * h * h))
    value = 0.5 * h * (1.0 + t)
    slope = 0.5 * (1.0 + t) + 0.5 * h * (1.0 - t * t) * c * (1.0 + 3.0 * 0.044715 * h * h)
    return (value, slope)


def token_contract(left, right):
    return lax.dot_general(
        left, right, (((0,), (0,)), ((), ())), preferred_element_type=jnp.float32
    )


def width_contract(left, right):
    return lax.dot_general(
        left, right, (((1,), (1,)), ((), ())), preferred_element_type=jnp.float32
    )


class ColGather:
    def __init__(self, n, own, panel, sems):
        self.lines = n // 2
        me = lax.axis_index("col")
        self.z, self.x = me // 2, me % 2
        self.own, self.panel = own, panel
        self.rows = own.shape[0]
        self.local, self.up, self.down, self.across, self.from_line, self.from_mate = sems

    def block(self, z, x):
        return self.panel.at[pl.ds((z * 2 + x) * self.rows, self.rows)]

    def copy(self, src, z, send, recv, target):
        return pltpu.make_async_remote_copy(
            src_ref=src, dst_ref=self.block(z, self.x), send_sem=send.at[z], recv_sem=recv.at[z],
            device_id={"col": target}, device_id_type=MESH,
        )

    def up_copy(self, z, src):
        return self.copy(src, z, self.up, self.from_line, (self.z + 1) * 2 + self.x)

    def down_copy(self, z, src):
        return self.copy(src, z, self.down, self.from_line, (self.z - 1) * 2 + self.x)

    def across_copy(self, z, src):
        return self.copy(src, z, self.across, self.from_mate, self.z * 2 + 1 - self.x)

    def start(self):
        pltpu.make_async_copy(self.own, self.block(self.z, self.x), self.local.at[0]).start()

        @pl.when(self.z < self.lines - 1)
        def _():
            self.up_copy(self.z, self.own).start()

        @pl.when(self.z > 0)
        def _():
            self.down_copy(self.z, self.own).start()

        self.across_copy(self.z, self.own).start()

    def wait_line(self, z):
        block = self.block(z, self.x)
        self.copy(block, z, self.up, self.from_line, self.z * 2 + 1 - self.x).wait_recv()

    def wait_mate(self, z):
        block = self.block(z, 1 - self.x)
        pltpu.make_async_remote_copy(
            src_ref=block, dst_ref=block, send_sem=self.across.at[z], recv_sem=self.from_mate.at[z],
            device_id={"col": self.z * 2 + 1 - self.x}, device_id_type=MESH,
        ).wait_recv()

    def step(self, s):
        @pl.when(self.z >= s)
        def _():
            z = self.z - s
            self.wait_line(z)
            self.across_copy(z, self.block(z, self.x)).start()

            @pl.when(self.z < self.lines - 1)
            def _():
                self.up_copy(z, self.block(z, self.x)).start()

        @pl.when(self.z + s < self.lines)
        def _():
            z = self.z + s
            self.wait_line(z)
            self.across_copy(z, self.block(z, self.x)).start()

            @pl.when(self.z > 0)
            def _():
                self.down_copy(z, self.block(z, self.x)).start()

    def wait_own(self):
        pltpu.make_async_copy(self.own, self.block(self.z, self.x), self.local.at[0]).wait()

    def end(self):
        for s in range(self.lines):
            @pl.when(self.z >= s)
            def _():
                z = self.z - s
                self.across_copy(z, self.block(z, self.x)).wait_send()

                @pl.when(self.z < self.lines - 1)
                def _():
                    self.up_copy(z, self.block(z, self.x)).wait_send()

            @pl.when(self.z + s < self.lines)
            def _():
                z = self.z + s
                if s > 0:
                    self.across_copy(z, self.block(z, self.x)).wait_send()

                @pl.when(self.z > 0)
                def _():
                    self.down_copy(z, self.block(z, self.x)).wait_send()


class RowGather:
    def __init__(self, n, own, panel, sems):
        self.outer = n // 2
        me = lax.axis_index("row")
        self.o, self.c = me // 2, me % 2
        self.own, self.panel = own, panel
        self.rows = own.shape[0]
        self.local, self.far, self.across, self.from_far, self.from_mate = sems

    def block(self, o, c):
        return self.panel.at[pl.ds((o * 2 + c) * self.rows, self.rows)]

    def far_copy(self, o):
        return pltpu.make_async_remote_copy(
            src_ref=self.own, dst_ref=self.block(self.o, self.c), send_sem=self.far.at[o],
            recv_sem=self.from_far.at[self.o], device_id={"row": o * 2 + self.c}, device_id_type=MESH,
        )

    def across_copy(self, o, src):
        return pltpu.make_async_remote_copy(
            src_ref=src, dst_ref=self.block(o, self.c), send_sem=self.across.at[o],
            recv_sem=self.from_mate.at[o], device_id={"row": self.o * 2 + 1 - self.c}, device_id_type=MESH,
        )

    def start(self):
        for k in range(1, self.outer):
            self.far_copy((self.o + k) % self.outer).start()
        self.across_copy(self.o, self.own).start()
        pltpu.make_async_copy(self.own, self.block(self.o, self.c), self.local.at[0]).start()

    def forward(self):
        for k in range(1, self.outer):
            o = (self.o + self.outer - k) % self.outer
            block = self.block(o, self.c)
            pltpu.make_async_remote_copy(
                src_ref=block, dst_ref=block, send_sem=self.far.at[o], recv_sem=self.from_far.at[o],
                device_id={"row": o * 2 + self.c}, device_id_type=MESH,
            ).wait_recv()
            self.across_copy(o, block).start()

    def end(self):
        pltpu.make_async_copy(self.own, self.block(self.o, self.c), self.local.at[0]).wait()
        for k in range(1, self.outer):
            self.far_copy((self.o + k) % self.outer).wait_send()
        for k in range(self.outer):
            o = (self.o + k) % self.outer
            self.across_copy(o, self.block(o, self.c)).wait_send()
            block = self.block(o, 1 - self.c)
            pltpu.make_async_remote_copy(
                src_ref=block, dst_ref=block, send_sem=self.across.at[o], recv_sem=self.from_mate.at[o],
                device_id={"row": self.o * 2 + 1 - self.c}, device_id_type=MESH,
            ).wait_recv()


def col_sems(n):
    lines = n // 2
    return [pltpu.SemaphoreType.DMA((1,))] + [pltpu.SemaphoreType.DMA((lines,))] * 5


def row_sems(n):
    return [pltpu.SemaphoreType.DMA((1,))] + [pltpu.SemaphoreType.DMA((n // 2,))] * 4


def greet(rows, cols):
    barrier = pltpu.get_barrier_semaphore()
    me_r, me_c = lax.axis_index("row"), lax.axis_index("col")
    outer, lines = rows // 2, cols // 2
    o, c, z, x = me_r // 2, me_r % 2, me_c // 2, me_c % 2
    count = 0
    if rows:
        for k in range(1, outer):
            pl.semaphore_signal(
                barrier, inc=1, device_id={"row": ((o + k) % outer) * 2 + c}, device_id_type=MESH
            )
        pl.semaphore_signal(barrier, inc=1, device_id={"row": o * 2 + 1 - c}, device_id_type=MESH)
        count = outer
    pl.semaphore_signal(barrier, inc=1, device_id={"col": z * 2 + 1 - x}, device_id_type=MESH)

    @pl.when(z > 0)
    def _():
        pl.semaphore_signal(barrier, inc=1, device_id={"col": (z - 1) * 2 + x}, device_id_type=MESH)

    @pl.when(z < lines - 1)
    def _():
        pl.semaphore_signal(barrier, inc=1, device_id={"col": (z + 1) * 2 + x}, device_id_type=MESH)

    count = count + 1 + jnp.where(z > 0, 1, 0) + jnp.where(z < lines - 1, 1, 0)
    pl.semaphore_wait(barrier, count)


STRIP = 16
COLS = 256


def hidden_kernel(
    n_row, n_col,
    li_ref, og_ref, pre_ref, wo_ref,
    li_panel, og_panel, act_panel, gp_panel,
    wo, pair, part, pre, act, slope, first, second, outgoing, own_gp,
    load_sem, s1_send, s1_recv, s2_send, s2_recv, *sems,
):
    og = ColGather(n_col, og_ref, og_panel, sems[0:6])
    li = ColGather(n_col, li_ref, li_panel, sems[6:12])
    act_rows = RowGather(n_row, act, act_panel, sems[12:17])
    gp_rows = RowGather(n_row, own_gp, gp_panel, sems[17:22])
    lines, outer = n_col // 2, n_row // 2
    rows = pre_ref.shape[0]
    me = lax.axis_index("row")
    o, c = me // 2, me % 2

    greet(n_row, n_col)
    og.start()
    load_pre = pltpu.make_async_copy(pre_ref, pre, load_sem.at[0])
    load_pre.start()
    load_wo = pltpu.make_async_copy(wo_ref, wo, load_sem.at[1])
    load_wo.start()

    load_pre.wait()

    @pl.loop(0, rows // STRIP)
    def _(i):
        r = pl.ds(pl.multiple_of(i * STRIP, STRIP), STRIP)
        v, d = gelu_parts(pre[r, :].astype(F32))
        act[r, :] = v.astype(BF16)
        slope[r, :] = d

    act_rows.start()
    load_wo.wait()
    og.wait_own()

    def multiply(z):
        size = 2 * og.rows
        start = pl.multiple_of(z * size, size)
        og.wait_mate(z)
        fetch = pltpu.make_async_copy(og_panel.at[pl.ds(start, size)], pair, load_sem.at[2])
        fetch.start()
        fetch.wait()

        @pl.loop(0, wo.shape[0] // COLS)
        def _(j):
            k = pl.ds(pl.multiple_of(j * COLS, COLS), COLS)
            part[pl.ds(start, size), k] = width_contract(pair[...], wo[k, :]).astype(BF16)

    def multiply_step(s):
        if s == 0:
            multiply(og.z)
        else:
            pl.when(og.z >= s)(lambda: multiply(og.z - s))
            pl.when(og.z + s < lines)(lambda: multiply(og.z + s))

    for s in range(1, lines):
        og.step(s)
        if s == lines - 1:
            li.start()
        multiply_step(s - 1)
    act_rows.forward()
    multiply_step(lines - 1)

    def own_rows(q):
        return pl.ds(pl.multiple_of(q * rows, rows), rows)

    def first_copy(k):
        return pltpu.make_async_remote_copy(
            src_ref=part.at[own_rows(k * 2 + 1 - c)], dst_ref=first.at[k], send_sem=s1_send.at[k],
            recv_sem=s1_recv.at[k], device_id={"row": o * 2 + 1 - c}, device_id_type=MESH,
        )

    def second_copy(k):
        return pltpu.make_async_remote_copy(
            src_ref=outgoing.at[k], dst_ref=second.at[o], send_sem=s2_send.at[k],
            recv_sem=s2_recv.at[o], device_id={"row": k * 2 + c}, device_id_type=MESH,
        )

    order = [(o + k) % outer for k in range(1, outer)] + [o]
    for k in order:
        first_copy(k).start()
    for k in order[:-1]:
        first_copy(k).wait_recv()

        @pl.loop(0, rows // STRIP)
        def _(i):
            at = pl.multiple_of(i * STRIP, STRIP)
            mine = part[pl.ds(pl.multiple_of((k * 2 + c) * rows + at, STRIP), STRIP), :]
            r = pl.ds(at, STRIP)
            outgoing[k, r, :] = (mine.astype(F32) + first[k, r, :].astype(F32)).astype(BF16)

        second_copy(k).start()

    li.wait_own()
    steps = list(range(1, lines))
    early = steps[: max(1, len(steps) // 3)]
    for s in early:
        li.step(s)

    first_copy(o).wait_recv()
    for k in order[:-1]:
        pltpu.make_async_remote_copy(
            src_ref=outgoing.at[k], dst_ref=second.at[k], send_sem=s2_send.at[k],
            recv_sem=s2_recv.at[k], device_id={"row": k * 2 + c}, device_id_type=MESH,
        ).wait_recv()

    @pl.loop(0, rows // STRIP)
    def _(i):
        at = pl.multiple_of(i * STRIP, STRIP)
        r = pl.ds(at, STRIP)
        total = part[pl.ds(pl.multiple_of(me * rows + at, STRIP), STRIP), :].astype(F32)
        total = total + first[o, r, :].astype(F32)
        for k in order[:-1]:
            total = total + second[k, r, :].astype(F32)
        own_gp[r, :] = (total * slope[r, :]).astype(BF16)

    gp_rows.start()
    for s in steps[len(early):]:
        li.step(s)
    gp_rows.forward()

    for k in order:
        first_copy(k).wait_send()
    for k in order[:-1]:
        second_copy(k).wait_send()
    act_rows.end()
    gp_rows.end()
    og.end()
    for s in range(lines):
        if s == 0:
            li.wait_mate(li.z)
        else:
            pl.when(li.z >= s)(lambda: li.wait_mate(li.z - s))
            pl.when(li.z + s < lines)(lambda: li.wait_mate(li.z + s))
    li.end()


def hidden(n_row, n_col, layer_input, out_grad, preact, weight_out):
    t, d = layer_input.shape
    rows, f = preact.shape
    tokens = t * n_col
    outer = n_row // 2
    any_spec = pl.BlockSpec(memory_space=pl.ANY)
    return pl.pallas_call(
        functools.partial(hidden_kernel, n_row, n_col),
        out_shape=[
            jax.ShapeDtypeStruct((tokens, d), BF16),
            jax.ShapeDtypeStruct((tokens, d), BF16),
            jax.ShapeDtypeStruct((tokens, f), BF16),
            jax.ShapeDtypeStruct((tokens, f), BF16),
        ],
        in_specs=[any_spec] * 4,
        out_specs=[any_spec] * 4,
        scratch_shapes=[
            pltpu.VMEM((f, d), BF16),
            pltpu.VMEM((2 * t, d), BF16),
            pltpu.VMEM((tokens, f), BF16),
            pltpu.VMEM((rows, f), BF16),
            pltpu.VMEM((rows, f), BF16),
            pltpu.VMEM((rows, f), F32),
            pltpu.VMEM((outer, rows, f), BF16),
            pltpu.VMEM((outer, rows, f), BF16),
            pltpu.VMEM((outer, rows, f), BF16),
            pltpu.VMEM((rows, f), BF16),
            pltpu.SemaphoreType.DMA((3,)),
        ]
        + [pltpu.SemaphoreType.DMA((outer,))] * 4
        + col_sems(n_col) * 2
        + row_sems(n_row) * 2,
        compiler_params=pltpu.CompilerParams(
            collective_id=0, has_side_effects=True, vmem_limit_bytes=50 * 2**20
        ),
        cost_estimate=pl.CostEstimate(
            flops=2 * tokens * d * f, bytes_accessed=2 * (f * d + 4 * tokens * (d + f)), transcendentals=rows * f
        ),
        name="hidden",
    )(layer_input, out_grad, preact, weight_out)


def local(n_row, n_col, layer_input, out_grad, preact, weight_in, weight_out):
    li_panel, og_panel, act_panel, gp_panel = hidden(
        n_row, n_col, layer_input, out_grad, preact, weight_out
    )
    input_grad = lax.psum_scatter(
        width_contract(gp_panel, weight_in).astype(BF16), "col", scatter_dimension=0, tiled=True
    )
    weight_out_grad = token_contract(act_panel, og_panel)
    weight_in_grad = token_contract(li_panel, gp_panel)
    return (input_grad, weight_in_grad, weight_out_grad)


def solution(mesh):
    placed = (P("col", "row"), P("col", "row"), P("row", "col"), P("row", "col"), P("col", "row"))
    return jax.shard_map(
        functools.partial(local, mesh.shape["row"], mesh.shape["col"]),
        mesh=mesh,
        in_specs=placed,
        out_specs=(P("col", "row"), P("row", "col"), P("col", "row")),
        check_vma=False,
    )
```

```python
import functools
import math

import jax
import jax.numpy as jnp
import numpy as np
from jax import lax
from jax.experimental import pallas as pl
from jax.experimental.pallas import tpu as pltpu
from jax.sharding import PartitionSpec as P

MESH = pl.DeviceIdType.MESH
BF16 = jnp.bfloat16
F32 = jnp.float32
PIECES = 2


def gelu_parts(h):
    c = math.sqrt(2.0 / math.pi)
    t = jnp.tanh(c * (h + 0.044715 * h * h * h))
    value = 0.5 * h * (1.0 + t)
    slope = 0.5 * (1.0 + t) + 0.5 * h * (1.0 - t * t) * c * (1.0 + 3.0 * 0.044715 * h * h)
    return (value, slope)


def token_contract(left, right):
    return lax.dot_general(
        left, right, (((0,), (0,)), ((), ())), preferred_element_type=jnp.float32
    )


def width_contract(left, right):
    return lax.dot_general(
        left, right, (((1,), (1,)), ((), ())), preferred_element_type=jnp.float32
    )


class ColGather:
    def __init__(self, n, own, panel, sems):
        self.lines = n // 2
        me = lax.axis_index("col")
        self.z, self.x = me // 2, me % 2
        self.own, self.panel = own, panel
        self.rows = own.shape[0]
        self.size = self.rows // PIECES
        self.local, self.up, self.down, self.across, self.from_line, self.from_mate = sems

    def block(self, z, x, h):
        return self.panel.at[pl.ds((z * 2 + x) * self.rows + h * self.size, self.size)]

    def source(self, z, h, mine):
        return self.own.at[pl.ds(h * self.size, self.size)] if mine else self.block(z, self.x, h)

    def copy(self, src, z, h, send, recv, target):
        return pltpu.make_async_remote_copy(
            src_ref=src, dst_ref=self.block(z, self.x, h), send_sem=send.at[z * PIECES + h],
            recv_sem=recv.at[z * PIECES + h], device_id={"col": target}, device_id_type=MESH,
        )

    def up_copy(self, z, h, mine=False):
        return self.copy(self.source(z, h, mine), z, h, self.up, self.from_line, (self.z + 1) * 2 + self.x)

    def down_copy(self, z, h, mine=False):
        return self.copy(self.source(z, h, mine), z, h, self.down, self.from_line, (self.z - 1) * 2 + self.x)

    def across_copy(self, z, h, mine=False):
        return self.copy(self.source(z, h, mine), z, h, self.across, self.from_mate, self.z * 2 + 1 - self.x)

    def own_copy(self):
        return pltpu.make_async_copy(
            self.own, self.panel.at[pl.ds((self.z * 2 + self.x) * self.rows, self.rows)], self.local.at[0]
        )

    def start(self):
        for h in range(PIECES):
            pl.when(self.z < self.lines - 1)(lambda: self.up_copy(self.z, h, True).start())
            pl.when(self.z > 0)(lambda: self.down_copy(self.z, h, True).start())
            self.across_copy(self.z, h, True).start()
        self.own_copy().start()

    def wait_line(self, z, h):
        self.copy(
            self.block(z, self.x, h), z, h, self.up, self.from_line, self.z * 2 + 1 - self.x
        ).wait_recv()

    def wait_mate(self, z):
        for h in range(PIECES):
            block = self.block(z, 1 - self.x, h)
            pltpu.make_async_remote_copy(
                src_ref=block, dst_ref=block, send_sem=self.across.at[z * PIECES + h],
                recv_sem=self.from_mate.at[z * PIECES + h],
                device_id={"col": self.z * 2 + 1 - self.x}, device_id_type=MESH,
            ).wait_recv()

    def step(self, s):
        for h in range(PIECES):
            @pl.when(self.z >= s)
            def _():
                z = self.z - s
                self.wait_line(z, h)
                pl.when(self.z < self.lines - 1)(lambda: self.up_copy(z, h).start())
                self.across_copy(z, h).start()

            @pl.when(self.z + s < self.lines)
            def _():
                z = self.z + s
                self.wait_line(z, h)
                pl.when(self.z > 0)(lambda: self.down_copy(z, h).start())
                self.across_copy(z, h).start()

    def wait_own(self):
        self.own_copy().wait()

    def end(self):
        for s in range(self.lines):
            for h in range(PIECES):
                @pl.when(self.z >= s)
                def _():
                    z = self.z - s
                    self.across_copy(z, h).wait_send()
                    pl.when(self.z < self.lines - 1)(lambda: self.up_copy(z, h).wait_send())

                @pl.when(self.z + s < self.lines)
                def _():
                    z = self.z + s
                    if s > 0:
                        self.across_copy(z, h).wait_send()
                    pl.when(self.z > 0)(lambda: self.down_copy(z, h).wait_send())


class RowGather:
    def __init__(self, n, own, panel, sems):
        self.outer = n // 2
        me = lax.axis_index("row")
        self.o, self.c = me // 2, me % 2
        self.own, self.panel = own, panel
        self.rows = own.shape[0]
        self.local, self.far, self.across, self.from_far, self.from_mate = sems

    def block(self, o, c):
        return self.panel.at[pl.ds((o * 2 + c) * self.rows, self.rows)]

    def far_copy(self, o):
        return pltpu.make_async_remote_copy(
            src_ref=self.own, dst_ref=self.block(self.o, self.c), send_sem=self.far.at[o],
            recv_sem=self.from_far.at[self.o], device_id={"row": o * 2 + self.c}, device_id_type=MESH,
        )

    def across_copy(self, o, src):
        return pltpu.make_async_remote_copy(
            src_ref=src, dst_ref=self.block(o, self.c), send_sem=self.across.at[o],
            recv_sem=self.from_mate.at[o], device_id={"row": self.o * 2 + 1 - self.c}, device_id_type=MESH,
        )

    def start(self):
        for k in range(1, self.outer):
            self.far_copy((self.o + k) % self.outer).start()
        self.across_copy(self.o, self.own).start()
        pltpu.make_async_copy(self.own, self.block(self.o, self.c), self.local.at[0]).start()

    def forward(self):
        for k in range(1, self.outer):
            o = (self.o + self.outer - k) % self.outer
            block = self.block(o, self.c)
            pltpu.make_async_remote_copy(
                src_ref=block, dst_ref=block, send_sem=self.far.at[o], recv_sem=self.from_far.at[o],
                device_id={"row": o * 2 + self.c}, device_id_type=MESH,
            ).wait_recv()
            self.across_copy(o, block).start()

    def end(self):
        pltpu.make_async_copy(self.own, self.block(self.o, self.c), self.local.at[0]).wait()
        for k in range(1, self.outer):
            self.far_copy((self.o + k) % self.outer).wait_send()
        for k in range(self.outer):
            o = (self.o + k) % self.outer
            self.across_copy(o, self.block(o, self.c)).wait_send()
            block = self.block(o, 1 - self.c)
            pltpu.make_async_remote_copy(
                src_ref=block, dst_ref=block, send_sem=self.across.at[o], recv_sem=self.from_mate.at[o],
                device_id={"row": self.o * 2 + 1 - self.c}, device_id_type=MESH,
            ).wait_recv()


def col_sems(n):
    lines = n // 2
    return [pltpu.SemaphoreType.DMA((1,))] + [pltpu.SemaphoreType.DMA((lines * PIECES,))] * 5


def row_sems(n):
    return [pltpu.SemaphoreType.DMA((1,))] + [pltpu.SemaphoreType.DMA((n // 2,))] * 4


def greet(rows, cols):
    barrier = pltpu.get_barrier_semaphore()
    me_r, me_c = lax.axis_index("row"), lax.axis_index("col")
    outer, lines = rows // 2, cols // 2
    o, c, z, x = me_r // 2, me_r % 2, me_c // 2, me_c % 2
    count = 0
    if rows:
        for k in range(1, outer):
            pl.semaphore_signal(
                barrier, inc=1, device_id={"row": ((o + k) % outer) * 2 + c}, device_id_type=MESH
            )
        pl.semaphore_signal(barrier, inc=1, device_id={"row": o * 2 + 1 - c}, device_id_type=MESH)
        count = outer
    pl.semaphore_signal(barrier, inc=1, device_id={"col": z * 2 + 1 - x}, device_id_type=MESH)

    @pl.when(z > 0)
    def _():
        pl.semaphore_signal(barrier, inc=1, device_id={"col": (z - 1) * 2 + x}, device_id_type=MESH)

    @pl.when(z < lines - 1)
    def _():
        pl.semaphore_signal(barrier, inc=1, device_id={"col": (z + 1) * 2 + x}, device_id_type=MESH)

    count = count + 1 + jnp.where(z > 0, 1, 0) + jnp.where(z < lines - 1, 1, 0)
    pl.semaphore_wait(barrier, count)


STRIP = 16
COLS = 256


def hidden_kernel(
    n_row, n_col,
    li_ref, og_ref, pre_ref, wo_ref,
    li_panel, og_panel, act_panel, gp_panel,
    wo, pair, part, pre, act, slope, first, second, outgoing, own_gp,
    load_sem, s1_send, s1_recv, s2_send, s2_recv, *sems,
):
    og = ColGather(n_col, og_ref, og_panel, sems[0:6])
    li = ColGather(n_col, li_ref, li_panel, sems[6:12])
    act_rows = RowGather(n_row, act, act_panel, sems[12:17])
    gp_rows = RowGather(n_row, own_gp, gp_panel, sems[17:22])
    lines, outer = n_col // 2, n_row // 2
    rows = pre_ref.shape[0]
    me = lax.axis_index("row")
    o, c = me // 2, me % 2

    greet(n_row, n_col)
    og.start()
    load_pre = pltpu.make_async_copy(pre_ref, pre, load_sem.at[0])
    load_pre.start()
    load_wo = pltpu.make_async_copy(wo_ref, wo, load_sem.at[1])
    load_wo.start()

    load_pre.wait()

    @pl.loop(0, rows // STRIP)
    def _(i):
        r = pl.ds(pl.multiple_of(i * STRIP, STRIP), STRIP)
        v, d = gelu_parts(pre[r, :].astype(F32))
        act[r, :] = v.astype(BF16)
        slope[r, :] = d

    act_rows.start()
    load_wo.wait()
    og.wait_own()

    def multiply(z):
        size = 2 * og.rows
        start = pl.multiple_of(z * size, size)
        og.wait_mate(z)
        fetch = pltpu.make_async_copy(og_panel.at[pl.ds(start, size)], pair, load_sem.at[2])
        fetch.start()
        fetch.wait()

        @pl.loop(0, wo.shape[0] // COLS)
        def _(j):
            k = pl.ds(pl.multiple_of(j * COLS, COLS), COLS)
            part[pl.ds(start, size), k] = width_contract(pair[...], wo[k, :]).astype(BF16)

    def multiply_step(s):
        if s == 0:
            multiply(og.z)
        else:
            pl.when(og.z >= s)(lambda: multiply(og.z - s))
            pl.when(og.z + s < lines)(lambda: multiply(og.z + s))

    for s in range(1, lines):
        og.step(s)
        if s == lines - 1:
            li.start()
        multiply_step(s - 1)
    act_rows.forward()
    multiply_step(lines - 1)

    def own_rows(q):
        return pl.ds(pl.multiple_of(q * rows, rows), rows)

    def first_copy(k):
        return pltpu.make_async_remote_copy(
            src_ref=part.at[own_rows(k * 2 + 1 - c)], dst_ref=first.at[k], send_sem=s1_send.at[k],
            recv_sem=s1_recv.at[k], device_id={"row": o * 2 + 1 - c}, device_id_type=MESH,
        )

    def second_copy(k):
        return pltpu.make_async_remote_copy(
            src_ref=outgoing.at[k], dst_ref=second.at[o], send_sem=s2_send.at[k],
            recv_sem=s2_recv.at[o], device_id={"row": k * 2 + c}, device_id_type=MESH,
        )

    order = [(o + k) % outer for k in range(1, outer)] + [o]
    for k in order:
        first_copy(k).start()
    for k in order[:-1]:
        first_copy(k).wait_recv()

        @pl.loop(0, rows // STRIP)
        def _(i):
            at = pl.multiple_of(i * STRIP, STRIP)
            mine = part[pl.ds(pl.multiple_of((k * 2 + c) * rows + at, STRIP), STRIP), :]
            r = pl.ds(at, STRIP)
            outgoing[k, r, :] = (mine.astype(F32) + first[k, r, :].astype(F32)).astype(BF16)

        second_copy(k).start()

    li.wait_own()
    steps = list(range(1, lines))
    early = steps[: max(1, 2 * len(steps) // 3)]
    for s in early:
        li.step(s)

    first_copy(o).wait_recv()
    for k in order[:-1]:
        pltpu.make_async_remote_copy(
            src_ref=outgoing.at[k], dst_ref=second.at[k], send_sem=s2_send.at[k],
            recv_sem=s2_recv.at[k], device_id={"row": k * 2 + c}, device_id_type=MESH,
        ).wait_recv()

    @pl.loop(0, rows // STRIP)
    def _(i):
        at = pl.multiple_of(i * STRIP, STRIP)
        r = pl.ds(at, STRIP)
        total = part[pl.ds(pl.multiple_of(me * rows + at, STRIP), STRIP), :].astype(F32)
        total = total + first[o, r, :].astype(F32)
        for k in order[:-1]:
            total = total + second[k, r, :].astype(F32)
        own_gp[r, :] = (total * slope[r, :]).astype(BF16)

    gp_rows.start()
    for s in steps[len(early):]:
        li.step(s)
    gp_rows.forward()

    for k in order:
        first_copy(k).wait_send()
    for k in order[:-1]:
        second_copy(k).wait_send()
    act_rows.end()
    gp_rows.end()
    og.end()
    for s in range(lines):
        if s == 0:
            li.wait_mate(li.z)
        else:
            pl.when(li.z >= s)(lambda: li.wait_mate(li.z - s))
            pl.when(li.z + s < lines)(lambda: li.wait_mate(li.z + s))
    li.end()


def hidden(n_row, n_col, layer_input, out_grad, preact, weight_out):
    t, d = layer_input.shape
    rows, f = preact.shape
    tokens = t * n_col
    outer = n_row // 2
    any_spec = pl.BlockSpec(memory_space=pltpu.HBM)
    return pl.pallas_call(
        functools.partial(hidden_kernel, n_row, n_col),
        out_shape=[
            jax.ShapeDtypeStruct((tokens, d), BF16),
            jax.ShapeDtypeStruct((tokens, d), BF16),
            jax.ShapeDtypeStruct((tokens, f), BF16),
            jax.ShapeDtypeStruct((tokens, f), BF16),
        ],
        in_specs=[any_spec] * 4,
        out_specs=[any_spec] * 4,
        scratch_shapes=[
            pltpu.VMEM((f, d), BF16),
            pltpu.VMEM((2 * t, d), BF16),
            pltpu.VMEM((tokens, f), BF16),
            pltpu.VMEM((rows, f), BF16),
            pltpu.VMEM((rows, f), BF16),
            pltpu.VMEM((rows, f), F32),
            pltpu.VMEM((outer, rows, f), BF16),
            pltpu.VMEM((outer, rows, f), BF16),
            pltpu.VMEM((outer, rows, f), BF16),
            pltpu.VMEM((rows, f), BF16),
            pltpu.SemaphoreType.DMA((3,)),
        ]
        + [pltpu.SemaphoreType.DMA((outer,))] * 4
        + col_sems(n_col) * 2
        + row_sems(n_row) * 2,
        compiler_params=pltpu.CompilerParams(
            collective_id=0, has_side_effects=True, vmem_limit_bytes=50 * 2**20
        ),
        cost_estimate=pl.CostEstimate(
            flops=2 * tokens * d * f, bytes_accessed=2 * (f * d + 4 * tokens * (d + f)), transcendentals=rows * f
        ),
        name="hidden",
    )(layer_input, out_grad, preact, weight_out)


def col_scatter(n_col, panel, weight):
    lines = n_col // 2
    me = lax.axis_index("col")
    z, x = me // 2, me % 2
    size = panel.shape[0] // lines
    rows = size // 2
    order = np.array([sorted(range(lines), key=lambda t: (-abs(t - p), t)) for p in range(lines)])
    place = np.argsort(order, axis=1)
    order, place = jnp.asarray(order, jnp.int32), jnp.asarray(place, jnp.int32)
    swap = [(i, i + 1 - 2 * (i % 2)) for i in range(n_col)]
    sums = []

    def of(target):
        at = place[z, jnp.clip(target, 0, lines - 1)]
        found = sums[0]
        for i in range(1, len(sums)):
            found = jnp.where(at == i, sums[i], found)
        return found.astype(F32)

    up = down = None
    for step in range(lines):
        block = lax.dynamic_slice_in_dim(panel, order[z, step] * size, size, 0)
        product = width_contract(block, weight).astype(BF16)
        away = lax.dynamic_slice_in_dim(product, (1 - x) * rows, rows, 0)
        keep = lax.dynamic_slice_in_dim(product, x * rows, rows, 0)
        got = lax.ppermute(away, "col", swap)
        sums.append((keep.astype(F32) + got.astype(F32)).astype(BF16))
        far = lines - 1 - step
        going_up, going_down = of(z + far), of(z - far)
        if step > 0:
            going_up, going_down = going_up + up.astype(F32), going_down + down.astype(F32)
        if far > 0:
            ups = [(2 * p + i, 2 * p + 2 + i) for p in range(step + 1) for i in range(2)]
            downs = [(n_col - 1 - a, n_col - 1 - b) for a, b in ups]
            up = lax.ppermute(going_up.astype(BF16), "col", ups)
            down = lax.ppermute(going_down.astype(BF16), "col", downs)
    return (going_up + down.astype(F32)).astype(BF16)


def local(n_row, n_col, layer_input, out_grad, preact, weight_in, weight_out):
    li_panel, og_panel, act_panel, gp_panel = hidden(
        n_row, n_col, layer_input, out_grad, preact, weight_out
    )
    input_grad = col_scatter(n_col, gp_panel, weight_in)
    weight_out_grad = token_contract(act_panel, og_panel)
    weight_in_grad = token_contract(li_panel, gp_panel)
    return (input_grad, weight_in_grad, weight_out_grad)


def solution(mesh):
    placed = (P("col", "row"), P("col", "row"), P("row", "col"), P("row", "col"), P("col", "row"))
    return jax.shard_map(
        functools.partial(local, mesh.shape["row"], mesh.shape["col"]),
        mesh=mesh,
        in_specs=placed,
        out_specs=(P("col", "row"), P("row", "col"), P("col", "row")),
        check_vma=False,
    )
```

```python
import functools
import math

import jax
import jax.numpy as jnp
import numpy as np
from jax import lax
from jax.experimental import pallas as pl
from jax.experimental.pallas import tpu as pltpu
from jax.sharding import PartitionSpec as P

MESH = pl.DeviceIdType.MESH
BF16 = jnp.bfloat16
F32 = jnp.float32
PIECES = 2


def gelu_parts(h):
    c = math.sqrt(2.0 / math.pi)
    t = jnp.tanh(c * (h + 0.044715 * h * h * h))
    value = 0.5 * h * (1.0 + t)
    slope = 0.5 * (1.0 + t) + 0.5 * h * (1.0 - t * t) * c * (1.0 + 3.0 * 0.044715 * h * h)
    return (value, slope)


def token_contract(left, right):
    return lax.dot_general(
        left, right, (((0,), (0,)), ((), ())), preferred_element_type=jnp.float32
    )


def width_contract(left, right):
    return lax.dot_general(
        left, right, (((1,), (1,)), ((), ())), preferred_element_type=jnp.float32
    )


class ColGather:
    def __init__(self, n, own, panel, sems):
        self.lines = n // 2
        me = lax.axis_index("col")
        self.z, self.x = me // 2, me % 2
        self.own, self.panel = own, panel
        self.rows = own.shape[0]
        self.size = self.rows // PIECES
        self.local, self.up, self.down, self.across, self.from_line, self.from_mate = sems

    def block(self, z, x, h):
        return self.panel.at[pl.ds((z * 2 + x) * self.rows + h * self.size, self.size)]

    def source(self, z, h, mine):
        return self.own.at[pl.ds(h * self.size, self.size)] if mine else self.block(z, self.x, h)

    def copy(self, src, z, h, send, recv, target):
        return pltpu.make_async_remote_copy(
            src_ref=src, dst_ref=self.block(z, self.x, h), send_sem=send.at[z * PIECES + h],
            recv_sem=recv.at[z * PIECES + h], device_id={"col": target}, device_id_type=MESH,
        )

    def up_copy(self, z, h, mine=False):
        return self.copy(self.source(z, h, mine), z, h, self.up, self.from_line, (self.z + 1) * 2 + self.x)

    def down_copy(self, z, h, mine=False):
        return self.copy(self.source(z, h, mine), z, h, self.down, self.from_line, (self.z - 1) * 2 + self.x)

    def across_copy(self, z, h, mine=False):
        return self.copy(self.source(z, h, mine), z, h, self.across, self.from_mate, self.z * 2 + 1 - self.x)

    def own_copy(self):
        return pltpu.make_async_copy(
            self.own, self.panel.at[pl.ds((self.z * 2 + self.x) * self.rows, self.rows)], self.local.at[0]
        )

    def start(self):
        for h in range(PIECES):
            pl.when(self.z < self.lines - 1)(lambda: self.up_copy(self.z, h, True).start())
            pl.when(self.z > 0)(lambda: self.down_copy(self.z, h, True).start())
            self.across_copy(self.z, h, True).start()
        self.own_copy().start()

    def wait_line(self, z, h):
        self.copy(
            self.block(z, self.x, h), z, h, self.up, self.from_line, self.z * 2 + 1 - self.x
        ).wait_recv()

    def wait_mate(self, z):
        for h in range(PIECES):
            block = self.block(z, 1 - self.x, h)
            pltpu.make_async_remote_copy(
                src_ref=block, dst_ref=block, send_sem=self.across.at[z * PIECES + h],
                recv_sem=self.from_mate.at[z * PIECES + h],
                device_id={"col": self.z * 2 + 1 - self.x}, device_id_type=MESH,
            ).wait_recv()

    def step(self, s):
        for h in range(PIECES):
            @pl.when(self.z >= s)
            def _():
                z = self.z - s
                self.wait_line(z, h)
                pl.when(self.z < self.lines - 1)(lambda: self.up_copy(z, h).start())
                self.across_copy(z, h).start()

            @pl.when(self.z + s < self.lines)
            def _():
                z = self.z + s
                self.wait_line(z, h)
                pl.when(self.z > 0)(lambda: self.down_copy(z, h).start())
                self.across_copy(z, h).start()

    def wait_own(self):
        self.own_copy().wait()

    def end(self):
        for s in range(self.lines):
            for h in range(PIECES):
                @pl.when(self.z >= s)
                def _():
                    z = self.z - s
                    self.across_copy(z, h).wait_send()
                    pl.when(self.z < self.lines - 1)(lambda: self.up_copy(z, h).wait_send())

                @pl.when(self.z + s < self.lines)
                def _():
                    z = self.z + s
                    if s > 0:
                        self.across_copy(z, h).wait_send()
                    pl.when(self.z > 0)(lambda: self.down_copy(z, h).wait_send())


class RowGather:
    def __init__(self, n, own, panel, sems):
        self.outer = n // 2
        me = lax.axis_index("row")
        self.o, self.c = me // 2, me % 2
        self.own, self.panel = own, panel
        self.rows = own.shape[0]
        self.local, self.far, self.across, self.from_far, self.from_mate = sems

    def block(self, o, c):
        return self.panel.at[pl.ds((o * 2 + c) * self.rows, self.rows)]

    def far_copy(self, o):
        return pltpu.make_async_remote_copy(
            src_ref=self.own, dst_ref=self.block(self.o, self.c), send_sem=self.far.at[o],
            recv_sem=self.from_far.at[self.o], device_id={"row": o * 2 + self.c}, device_id_type=MESH,
        )

    def across_copy(self, o, src):
        return pltpu.make_async_remote_copy(
            src_ref=src, dst_ref=self.block(o, self.c), send_sem=self.across.at[o],
            recv_sem=self.from_mate.at[o], device_id={"row": self.o * 2 + 1 - self.c}, device_id_type=MESH,
        )

    def start(self):
        for k in range(1, self.outer):
            self.far_copy((self.o + k) % self.outer).start()
        self.across_copy(self.o, self.own).start()
        pltpu.make_async_copy(self.own, self.block(self.o, self.c), self.local.at[0]).start()

    def forward(self):
        for k in range(1, self.outer):
            o = (self.o + self.outer - k) % self.outer
            block = self.block(o, self.c)
            pltpu.make_async_remote_copy(
                src_ref=block, dst_ref=block, send_sem=self.far.at[o], recv_sem=self.from_far.at[o],
                device_id={"row": o * 2 + self.c}, device_id_type=MESH,
            ).wait_recv()
            self.across_copy(o, block).start()

    def end(self):
        pltpu.make_async_copy(self.own, self.block(self.o, self.c), self.local.at[0]).wait()
        for k in range(1, self.outer):
            self.far_copy((self.o + k) % self.outer).wait_send()
        for k in range(self.outer):
            o = (self.o + k) % self.outer
            self.across_copy(o, self.block(o, self.c)).wait_send()
            block = self.block(o, 1 - self.c)
            pltpu.make_async_remote_copy(
                src_ref=block, dst_ref=block, send_sem=self.across.at[o], recv_sem=self.from_mate.at[o],
                device_id={"row": self.o * 2 + 1 - self.c}, device_id_type=MESH,
            ).wait_recv()


def col_sems(n):
    lines = n // 2
    return [pltpu.SemaphoreType.DMA((1,))] + [pltpu.SemaphoreType.DMA((lines * PIECES,))] * 5


def row_sems(n):
    return [pltpu.SemaphoreType.DMA((1,))] + [pltpu.SemaphoreType.DMA((n // 2,))] * 4


def greet(rows, cols):
    barrier = pltpu.get_barrier_semaphore()
    me_r, me_c = lax.axis_index("row"), lax.axis_index("col")
    outer, lines = rows // 2, cols // 2
    o, c, z, x = me_r // 2, me_r % 2, me_c // 2, me_c % 2
    count = 0
    if rows:
        for k in range(1, outer):
            pl.semaphore_signal(
                barrier, inc=1, device_id={"row": ((o + k) % outer) * 2 + c}, device_id_type=MESH
            )
        pl.semaphore_signal(barrier, inc=1, device_id={"row": o * 2 + 1 - c}, device_id_type=MESH)
        count = outer
    pl.semaphore_signal(barrier, inc=1, device_id={"col": z * 2 + 1 - x}, device_id_type=MESH)

    @pl.when(z > 0)
    def _():
        pl.semaphore_signal(barrier, inc=1, device_id={"col": (z - 1) * 2 + x}, device_id_type=MESH)

    @pl.when(z < lines - 1)
    def _():
        pl.semaphore_signal(barrier, inc=1, device_id={"col": (z + 1) * 2 + x}, device_id_type=MESH)

    count = count + 1 + jnp.where(z > 0, 1, 0) + jnp.where(z < lines - 1, 1, 0)
    pl.semaphore_wait(barrier, count)


STRIP = 16
COLS = 256
TALL = 512


def hidden_kernel(
    n_row, n_col,
    li_ref, og_ref, pre_ref, wi_ref, wo_ref,
    li_panel, og_panel, act_panel, gp_panel, out_panel,
    wi, wo, pair, part, product, pre, act, slope, first, second, outgoing, own_gp,
    load_sem, s1_send, s1_recv, s2_send, s2_recv, *sems,
):
    og = ColGather(n_col, og_ref, og_panel, sems[0:6])
    li = ColGather(n_col, li_ref, li_panel, sems[6:12])
    act_rows = RowGather(n_row, act, act_panel, sems[12:17])
    gp_rows = RowGather(n_row, own_gp, gp_panel, sems[17:22])
    lines, outer = n_col // 2, n_row // 2
    rows = pre_ref.shape[0]
    me = lax.axis_index("row")
    o, c = me // 2, me % 2

    greet(n_row, n_col)
    og.start()
    load_pre = pltpu.make_async_copy(pre_ref, pre, load_sem.at[0])
    load_pre.start()
    load_wo = pltpu.make_async_copy(wo_ref, wo, load_sem.at[1])
    load_wo.start()
    load_wi = pltpu.make_async_copy(wi_ref, wi, load_sem.at[3])
    load_wi.start()

    load_pre.wait()

    @pl.loop(0, rows // STRIP)
    def _(i):
        r = pl.ds(pl.multiple_of(i * STRIP, STRIP), STRIP)
        v, d = gelu_parts(pre[r, :].astype(F32))
        act[r, :] = v.astype(BF16)
        slope[r, :] = d

    act_rows.start()
    load_wo.wait()
    og.wait_own()

    def multiply(z):
        size = 2 * og.rows
        start = pl.multiple_of(z * size, size)
        og.wait_mate(z)
        fetch = pltpu.make_async_copy(og_panel.at[pl.ds(start, size)], pair, load_sem.at[2])
        fetch.start()
        fetch.wait()

        @pl.loop(0, wo.shape[0] // COLS)
        def _(j):
            k = pl.ds(pl.multiple_of(j * COLS, COLS), COLS)
            part[pl.ds(start, size), k] = width_contract(pair[...], wo[k, :]).astype(BF16)

    def own_rows(q):
        return pl.ds(pl.multiple_of(q * rows, rows), rows)

    def first_copy(k):
        return pltpu.make_async_remote_copy(
            src_ref=part.at[own_rows(k * 2 + 1 - c)], dst_ref=first.at[k], send_sem=s1_send.at[k],
            recv_sem=s1_recv.at[k], device_id={"row": o * 2 + 1 - c}, device_id_type=MESH,
        )

    def second_copy(k):
        return pltpu.make_async_remote_copy(
            src_ref=outgoing.at[k], dst_ref=second.at[o], send_sem=s2_send.at[k],
            recv_sem=s2_recv.at[o], device_id={"row": k * 2 + c}, device_id_type=MESH,
        )

    order = [(o + k) % outer for k in range(1, outer)] + [o]
    owners = 2 * og.rows // rows

    def exchange(z):
        for i in range(owners):
            q = z * owners + i
            k, kc = q // 2, q % 2
            pl.when(c != kc)(lambda: first_copy(k).start())
        for i in range(owners):
            q = z * owners + i
            k, kc = q // 2, q % 2

            @pl.when(c == kc)
            def _():
                first_copy(k).wait_recv()

                @pl.when(o != k)
                def _():
                    @pl.loop(0, rows // STRIP)
                    def _(i):
                        at = pl.multiple_of(i * STRIP, STRIP)
                        mine = part[pl.ds(pl.multiple_of(q * rows + at, STRIP), STRIP), :]
                        r = pl.ds(at, STRIP)
                        outgoing[k, r, :] = (mine.astype(F32) + first[k, r, :].astype(F32)).astype(BF16)

                    second_copy(k).start()

    def finish(z):
        @pl.when(me // owners == z)
        def _():
            for k in order[:-1]:
                pltpu.make_async_remote_copy(
                    src_ref=outgoing.at[k], dst_ref=second.at[k], send_sem=s2_send.at[k],
                    recv_sem=s2_recv.at[k], device_id={"row": k * 2 + c}, device_id_type=MESH,
                ).wait_recv()

            @pl.loop(0, rows // STRIP)
            def _(i):
                at = pl.multiple_of(i * STRIP, STRIP)
                r = pl.ds(at, STRIP)
                total = part[pl.ds(pl.multiple_of(me * rows + at, STRIP), STRIP), :].astype(F32)
                total = total + first[o, r, :].astype(F32)
                for k in order[:-1]:
                    total = total + second[k, r, :].astype(F32)
                own_gp[r, :] = (total * slope[r, :]).astype(BF16)

            gp_rows.start()

    def at_step(s, act_on):
        if s == 0:
            act_on(og.z)
        elif s > 0:
            pl.when(og.z >= s)(lambda: act_on(og.z - s))
            pl.when(og.z + s < lines)(lambda: act_on(og.z + s))

    def multiply_and_exchange(z):
        multiply(z)
        exchange(z)

    for s in range(1, lines):
        og.step(s)
        if s == lines - 1:
            li.start()
        at_step(s - 1, multiply_and_exchange)
        at_step(s - 2, finish)
    act_rows.forward()
    at_step(lines - 1, multiply_and_exchange)
    li.wait_own()
    steps = list(range(1, lines))
    early = steps[: max(1, 2 * len(steps) // 3)]
    li.step(1)
    at_step(lines - 2, finish)
    for s in early[1:]:
        li.step(s)
    at_step(lines - 1, finish)
    for s in steps[len(early):]:
        li.step(s)
    gp_rows.forward()
    for k in order:
        first_copy(k).wait_send()
    gp_rows.end()
    fetch_gp = pltpu.make_async_copy(gp_panel, part, load_sem.at[2])
    fetch_gp.start()
    load_wi.wait()
    fetch_gp.wait()

    @pl.loop(0, part.shape[0] // TALL)
    def _(i):
        r = pl.ds(pl.multiple_of(i * TALL, TALL), TALL)

        @pl.loop(0, wi.shape[0] // COLS)
        def _(j):
            k = pl.ds(pl.multiple_of(j * COLS, COLS), COLS)
            product[r, k] = width_contract(part[r, :], wi[k, :]).astype(BF16)

    store = pltpu.make_async_copy(product, out_panel, load_sem.at[2])
    store.start()

    for k in order[:-1]:
        second_copy(k).wait_send()
    act_rows.end()
    og.end()
    for s in range(lines):
        if s == 0:
            li.wait_mate(li.z)
        else:
            pl.when(li.z >= s)(lambda: li.wait_mate(li.z - s))
            pl.when(li.z + s < lines)(lambda: li.wait_mate(li.z + s))
    li.end()
    store.wait()


def hidden(n_row, n_col, layer_input, out_grad, preact, weight_in, weight_out):
    t, d = layer_input.shape
    rows, f = preact.shape
    tokens = t * n_col
    outer = n_row // 2
    any_spec = pl.BlockSpec(memory_space=pltpu.HBM)
    return pl.pallas_call(
        functools.partial(hidden_kernel, n_row, n_col),
        out_shape=[
            jax.ShapeDtypeStruct((tokens, d), BF16),
            jax.ShapeDtypeStruct((tokens, d), BF16),
            jax.ShapeDtypeStruct((tokens, f), BF16),
            jax.ShapeDtypeStruct((tokens, f), BF16),
            jax.ShapeDtypeStruct((tokens, d), BF16),
        ],
        in_specs=[any_spec] * 5,
        out_specs=[any_spec] * 5,
        scratch_shapes=[
            pltpu.VMEM((d, f), BF16),
            pltpu.VMEM((f, d), BF16),
            pltpu.VMEM((2 * t, d), BF16),
            pltpu.VMEM((tokens, f), BF16),
            pltpu.VMEM((tokens, d), BF16),
            pltpu.VMEM((rows, f), BF16),
            pltpu.VMEM((rows, f), BF16),
            pltpu.VMEM((rows, f), F32),
            pltpu.VMEM((outer, rows, f), BF16),
            pltpu.VMEM((outer, rows, f), BF16),
            pltpu.VMEM((outer, rows, f), BF16),
            pltpu.VMEM((rows, f), BF16),
            pltpu.SemaphoreType.DMA((4,)),
        ]
        + [pltpu.SemaphoreType.DMA((outer,))] * 4
        + col_sems(n_col) * 2
        + row_sems(n_row) * 2,
        compiler_params=pltpu.CompilerParams(
            collective_id=0, has_side_effects=True, vmem_limit_bytes=58 * 2**20
        ),
        cost_estimate=pl.CostEstimate(
            flops=4 * tokens * d * f, bytes_accessed=4 * (f * d + 2 * tokens * (d + f)), transcendentals=rows * f
        ),
        name="hidden",
    )(layer_input, out_grad, preact, weight_in, weight_out)


def col_scatter(n_col, panel, others):
    lines = n_col // 2
    me = lax.axis_index("col")
    z, x = me // 2, me % 2
    rows = panel.shape[0] // n_col
    order = np.array([sorted(range(lines), key=lambda t: (-abs(t - p), t)) for p in range(lines)])
    place = np.argsort(order, axis=1)
    order, place = jnp.asarray(order, jnp.int32), jnp.asarray(place, jnp.int32)
    swap = [(i, i + 1 - 2 * (i % 2)) for i in range(n_col)]
    sums = []

    def of(target):
        at = place[z, jnp.clip(target, 0, lines - 1)]
        found = sums[0]
        for i in range(1, len(sums)):
            found = jnp.where(at == i, sums[i], found)
        return found.astype(F32)

    up = down = None
    for step in range(lines):
        at = order[z, step] * 2
        away = lax.dynamic_slice_in_dim(panel, (at + 1 - x) * rows, rows, 0)
        keep = lax.dynamic_slice_in_dim(panel, (at + x) * rows, rows, 0)
        if step in others:
            keep, others[step] = lax.optimization_barrier((keep, others[step]))
        got = lax.ppermute(away, "col", swap)
        sums.append((keep.astype(F32) + got.astype(F32)).astype(BF16))
        far = lines - 1 - step
        going_up, going_down = of(z + far), of(z - far)
        if step > 0:
            going_up, going_down = going_up + up.astype(F32), going_down + down.astype(F32)
        if far > 0:
            ups = [(2 * p + i, 2 * p + 2 + i) for p in range(step + 1) for i in range(2)]
            downs = [(n_col - 1 - a, n_col - 1 - b) for a, b in ups]
            up = lax.ppermute(going_up.astype(BF16), "col", ups)
            down = lax.ppermute(going_down.astype(BF16), "col", downs)
    return (going_up + down.astype(F32)).astype(BF16), others


def local(n_row, n_col, layer_input, out_grad, preact, weight_in, weight_out):
    li_panel, og_panel, act_panel, gp_panel, out_panel = hidden(
        n_row, n_col, layer_input, out_grad, preact, weight_in, weight_out
    )
    beside = {0: token_contract(act_panel, og_panel), 2: token_contract(li_panel, gp_panel)}
    input_grad, beside = col_scatter(n_col, out_panel, beside)
    return (input_grad, beside[2], beside[0])


def solution(mesh):
    placed = (P("col", "row"), P("col", "row"), P("row", "col"), P("row", "col"), P("col", "row"))
    return jax.shard_map(
        functools.partial(local, mesh.shape["row"], mesh.shape["col"]),
        mesh=mesh,
        in_specs=placed,
        out_specs=(P("col", "row"), P("row", "col"), P("col", "row")),
        check_vma=False,
    )
```

```python
import functools
import math

import jax
import jax.numpy as jnp
import numpy as np
from jax import lax
from jax.experimental import pallas as pl
from jax.experimental.pallas import tpu as pltpu
from jax.sharding import PartitionSpec as P

MESH = pl.DeviceIdType.MESH
BF16 = jnp.bfloat16
F32 = jnp.float32
PIECES = 2


def gelu_parts(h):
    c = math.sqrt(2.0 / math.pi)
    t = jnp.tanh(c * (h + 0.044715 * h * h * h))
    value = 0.5 * h * (1.0 + t)
    slope = 0.5 * (1.0 + t) + 0.5 * h * (1.0 - t * t) * c * (1.0 + 3.0 * 0.044715 * h * h)
    return (value, slope)


def token_contract(left, right):
    return lax.dot_general(
        left, right, (((0,), (0,)), ((), ())), preferred_element_type=jnp.float32
    )


def width_contract(left, right):
    return lax.dot_general(
        left, right, (((1,), (1,)), ((), ())), preferred_element_type=jnp.float32
    )


class ColGather:
    def __init__(self, n, own, panel, sems):
        self.lines = n // 2
        me = lax.axis_index("col")
        self.z, self.x = me // 2, me % 2
        self.own, self.panel = own, panel
        self.rows = own.shape[0]
        self.size = self.rows // PIECES
        self.local, self.up, self.down, self.across, self.from_line, self.from_mate = sems

    def block(self, z, x, h):
        return self.panel.at[pl.ds((z * 2 + x) * self.rows + h * self.size, self.size)]

    def source(self, z, h, mine):
        return self.own.at[pl.ds(h * self.size, self.size)] if mine else self.block(z, self.x, h)

    def copy(self, src, z, h, send, recv, target):
        return pltpu.make_async_remote_copy(
            src_ref=src, dst_ref=self.block(z, self.x, h), send_sem=send.at[z * PIECES + h],
            recv_sem=recv.at[z * PIECES + h], device_id={"col": target}, device_id_type=MESH,
        )

    def up_copy(self, z, h, mine=False):
        return self.copy(self.source(z, h, mine), z, h, self.up, self.from_line, (self.z + 1) * 2 + self.x)

    def down_copy(self, z, h, mine=False):
        return self.copy(self.source(z, h, mine), z, h, self.down, self.from_line, (self.z - 1) * 2 + self.x)

    def across_copy(self, z, h, mine=False):
        return self.copy(self.source(z, h, mine), z, h, self.across, self.from_mate, self.z * 2 + 1 - self.x)

    def own_copy(self):
        return pltpu.make_async_copy(
            self.own, self.panel.at[pl.ds((self.z * 2 + self.x) * self.rows, self.rows)], self.local.at[0]
        )

    def start(self):
        for h in range(PIECES):
            pl.when(self.z < self.lines - 1)(lambda: self.up_copy(self.z, h, True).start())
            pl.when(self.z > 0)(lambda: self.down_copy(self.z, h, True).start())
            self.across_copy(self.z, h, True).start()
        self.own_copy().start()

    def wait_line(self, z, h):
        self.copy(
            self.block(z, self.x, h), z, h, self.up, self.from_line, self.z * 2 + 1 - self.x
        ).wait_recv()

    def wait_mate(self, z):
        for h in range(PIECES):
            block = self.block(z, 1 - self.x, h)
            pltpu.make_async_remote_copy(
                src_ref=block, dst_ref=block, send_sem=self.across.at[z * PIECES + h],
                recv_sem=self.from_mate.at[z * PIECES + h],
                device_id={"col": self.z * 2 + 1 - self.x}, device_id_type=MESH,
            ).wait_recv()

    def step(self, s):
        for h in range(PIECES):
            @pl.when(self.z >= s)
            def _():
                z = self.z - s
                self.wait_line(z, h)
                pl.when(self.z < self.lines - 1)(lambda: self.up_copy(z, h).start())
                self.across_copy(z, h).start()

            @pl.when(self.z + s < self.lines)
            def _():
                z = self.z + s
                self.wait_line(z, h)
                pl.when(self.z > 0)(lambda: self.down_copy(z, h).start())
                self.across_copy(z, h).start()

    def wait_own(self):
        self.own_copy().wait()

    def end(self):
        for s in range(self.lines):
            for h in range(PIECES):
                @pl.when(self.z >= s)
                def _():
                    z = self.z - s
                    self.across_copy(z, h).wait_send()
                    pl.when(self.z < self.lines - 1)(lambda: self.up_copy(z, h).wait_send())

                @pl.when(self.z + s < self.lines)
                def _():
                    z = self.z + s
                    if s > 0:
                        self.across_copy(z, h).wait_send()
                    pl.when(self.z > 0)(lambda: self.down_copy(z, h).wait_send())


class RowGather:
    def __init__(self, n, own, panel, sems):
        self.outer = n // 2
        me = lax.axis_index("row")
        self.o, self.c = me // 2, me % 2
        self.own, self.panel = own, panel
        self.rows = own.shape[0]
        self.local, self.far, self.across, self.from_far, self.from_mate = sems

    def block(self, o, c):
        return self.panel.at[pl.ds((o * 2 + c) * self.rows, self.rows)]

    def far_copy(self, o):
        return pltpu.make_async_remote_copy(
            src_ref=self.own, dst_ref=self.block(self.o, self.c), send_sem=self.far.at[o],
            recv_sem=self.from_far.at[self.o], device_id={"row": o * 2 + self.c}, device_id_type=MESH,
        )

    def across_copy(self, o, src):
        return pltpu.make_async_remote_copy(
            src_ref=src, dst_ref=self.block(o, self.c), send_sem=self.across.at[o],
            recv_sem=self.from_mate.at[o], device_id={"row": self.o * 2 + 1 - self.c}, device_id_type=MESH,
        )

    def start(self):
        for k in range(1, self.outer):
            self.far_copy((self.o + k) % self.outer).start()
        self.across_copy(self.o, self.own).start()
        pltpu.make_async_copy(self.own, self.block(self.o, self.c), self.local.at[0]).start()

    def forward(self):
        for k in range(1, self.outer):
            o = (self.o + self.outer - k) % self.outer
            block = self.block(o, self.c)
            pltpu.make_async_remote_copy(
                src_ref=block, dst_ref=block, send_sem=self.far.at[o], recv_sem=self.from_far.at[o],
                device_id={"row": o * 2 + self.c}, device_id_type=MESH,
            ).wait_recv()
            self.across_copy(o, block).start()

    def wait_own(self):
        pltpu.make_async_copy(self.own, self.block(self.o, self.c), self.local.at[0]).wait()

    def pass_on(self, o):
        block = self.block(o, self.c)
        pltpu.make_async_remote_copy(
            src_ref=block, dst_ref=block, send_sem=self.far.at[o], recv_sem=self.from_far.at[o],
            device_id={"row": o * 2 + self.c}, device_id_type=MESH,
        ).wait_recv()
        self.across_copy(o, block).start()

    def wait_mate(self, o):
        block = self.block(o, 1 - self.c)
        pltpu.make_async_remote_copy(
            src_ref=block, dst_ref=block, send_sem=self.across.at[o], recv_sem=self.from_mate.at[o],
            device_id={"row": self.o * 2 + 1 - self.c}, device_id_type=MESH,
        ).wait_recv()

    def wait_sends(self):
        for k in range(1, self.outer):
            self.far_copy((self.o + k) % self.outer).wait_send()
        for k in range(self.outer):
            o = (self.o + k) % self.outer
            self.across_copy(o, self.block(o, self.c)).wait_send()

    def end(self):
        self.wait_own()
        for k in range(1, self.outer):
            self.far_copy((self.o + k) % self.outer).wait_send()
        for k in range(self.outer):
            o = (self.o + k) % self.outer
            self.across_copy(o, self.block(o, self.c)).wait_send()
            block = self.block(o, 1 - self.c)
            pltpu.make_async_remote_copy(
                src_ref=block, dst_ref=block, send_sem=self.across.at[o], recv_sem=self.from_mate.at[o],
                device_id={"row": self.o * 2 + 1 - self.c}, device_id_type=MESH,
            ).wait_recv()


def col_sems(n):
    lines = n // 2
    return [pltpu.SemaphoreType.DMA((1,))] + [pltpu.SemaphoreType.DMA((lines * PIECES,))] * 5


def row_sems(n):
    return [pltpu.SemaphoreType.DMA((1,))] + [pltpu.SemaphoreType.DMA((n // 2,))] * 4


def greet(rows, cols):
    barrier = pltpu.get_barrier_semaphore()
    me_r, me_c = lax.axis_index("row"), lax.axis_index("col")
    outer, lines = rows // 2, cols // 2
    o, c, z, x = me_r // 2, me_r % 2, me_c // 2, me_c % 2
    count = 0
    if rows:
        for k in range(1, outer):
            pl.semaphore_signal(
                barrier, inc=1, device_id={"row": ((o + k) % outer) * 2 + c}, device_id_type=MESH
            )
        pl.semaphore_signal(barrier, inc=1, device_id={"row": o * 2 + 1 - c}, device_id_type=MESH)
        count = outer
    pl.semaphore_signal(barrier, inc=1, device_id={"col": z * 2 + 1 - x}, device_id_type=MESH)

    @pl.when(z > 0)
    def _():
        pl.semaphore_signal(barrier, inc=1, device_id={"col": (z - 1) * 2 + x}, device_id_type=MESH)

    @pl.when(z < lines - 1)
    def _():
        pl.semaphore_signal(barrier, inc=1, device_id={"col": (z + 1) * 2 + x}, device_id_type=MESH)

    count = count + 1 + jnp.where(z > 0, 1, 0) + jnp.where(z < lines - 1, 1, 0)
    pl.semaphore_wait(barrier, count)


STRIP = 16
COLS = 256


def hidden_kernel(
    n_row, n_col,
    li_ref, og_ref, pre_ref, wi_ref, wo_ref,
    li_panel, og_panel, act_panel, gp_panel, out_panel,
    wi, wo, pair, gp_pair, part, product, pre, act, slope, first, second, outgoing, own_gp,
    load_sem, s1_send, s1_recv, s2_send, s2_recv, *sems,
):
    og = ColGather(n_col, og_ref, og_panel, sems[0:6])
    li = ColGather(n_col, li_ref, li_panel, sems[6:12])
    act_rows = RowGather(n_row, act, act_panel, sems[12:17])
    gp_rows = RowGather(n_row, own_gp, gp_panel, sems[17:22])
    lines, outer = n_col // 2, n_row // 2
    rows = pre_ref.shape[0]
    me = lax.axis_index("row")
    o, c = me // 2, me % 2

    greet(n_row, n_col)
    og.start()
    load_pre = pltpu.make_async_copy(pre_ref, pre, load_sem.at[0])
    load_pre.start()
    load_wo = pltpu.make_async_copy(wo_ref, wo, load_sem.at[1])
    load_wo.start()
    load_wi = pltpu.make_async_copy(wi_ref, wi, load_sem.at[3])
    load_wi.start()

    load_pre.wait()

    @pl.loop(0, rows // STRIP)
    def _(i):
        r = pl.ds(pl.multiple_of(i * STRIP, STRIP), STRIP)
        v, d = gelu_parts(pre[r, :].astype(F32))
        act[r, :] = v.astype(BF16)
        slope[r, :] = d

    act_rows.start()
    load_wo.wait()
    og.wait_own()

    def multiply(z):
        size = 2 * og.rows
        start = pl.multiple_of(z * size, size)
        og.wait_mate(z)
        fetch = pltpu.make_async_copy(og_panel.at[pl.ds(start, size)], pair, load_sem.at[2])
        fetch.start()
        fetch.wait()

        @pl.loop(0, wo.shape[0] // COLS)
        def _(j):
            k = pl.ds(pl.multiple_of(j * COLS, COLS), COLS)
            part[pl.ds(start, size), k] = width_contract(pair[...], wo[k, :]).astype(BF16)

    def own_rows(q):
        return pl.ds(pl.multiple_of(q * rows, rows), rows)

    def first_copy(k):
        return pltpu.make_async_remote_copy(
            src_ref=part.at[own_rows(k * 2 + 1 - c)], dst_ref=first.at[k], send_sem=s1_send.at[k],
            recv_sem=s1_recv.at[k], device_id={"row": o * 2 + 1 - c}, device_id_type=MESH,
        )

    def second_copy(k):
        return pltpu.make_async_remote_copy(
            src_ref=outgoing.at[k], dst_ref=second.at[o], send_sem=s2_send.at[k],
            recv_sem=s2_recv.at[o], device_id={"row": k * 2 + c}, device_id_type=MESH,
        )

    order = [(o + k) % outer for k in range(1, outer)] + [o]
    owners = 2 * og.rows // rows

    def exchange(z):
        for i in range(owners):
            q = z * owners + i
            k, kc = q // 2, q % 2
            pl.when(c != kc)(lambda: first_copy(k).start())
        for i in range(owners):
            q = z * owners + i
            k, kc = q // 2, q % 2

            @pl.when(c == kc)
            def _():
                first_copy(k).wait_recv()

                @pl.when(o != k)
                def _():
                    @pl.loop(0, rows // STRIP)
                    def _(i):
                        at = pl.multiple_of(i * STRIP, STRIP)
                        mine = part[pl.ds(pl.multiple_of(q * rows + at, STRIP), STRIP), :]
                        r = pl.ds(at, STRIP)
                        outgoing[k, r, :] = (mine.astype(F32) + first[k, r, :].astype(F32)).astype(BF16)

                    second_copy(k).start()

    def finish(z):
        @pl.when(me // owners == z)
        def _():
            for k in order[:-1]:
                pltpu.make_async_remote_copy(
                    src_ref=outgoing.at[k], dst_ref=second.at[k], send_sem=s2_send.at[k],
                    recv_sem=s2_recv.at[k], device_id={"row": k * 2 + c}, device_id_type=MESH,
                ).wait_recv()

            @pl.loop(0, rows // STRIP)
            def _(i):
                at = pl.multiple_of(i * STRIP, STRIP)
                r = pl.ds(at, STRIP)
                total = part[pl.ds(pl.multiple_of(me * rows + at, STRIP), STRIP), :].astype(F32)
                total = total + first[o, r, :].astype(F32)
                for k in order[:-1]:
                    total = total + second[k, r, :].astype(F32)
                own_gp[r, :] = (total * slope[r, :]).astype(BF16)

            gp_rows.start()

    def at_step(s, act_on):
        if s == 0:
            act_on(og.z)
        elif s > 0:
            pl.when(og.z >= s)(lambda: act_on(og.z - s))
            pl.when(og.z + s < lines)(lambda: act_on(og.z + s))

    def multiply_and_exchange(z):
        multiply(z)
        exchange(z)

    for s in range(1, lines):
        og.step(s)
        if s == lines - 1:
            li.start()
        at_step(s - 1, multiply_and_exchange)
        at_step(s - 2, finish)
    act_rows.forward()
    at_step(lines - 1, multiply_and_exchange)
    def gp_ready(z):
        for i in range(owners):
            q = z * owners + i
            k, kc = q // 2, q % 2
            pl.when(q == me)(lambda: gp_rows.wait_own())
            pl.when((c == kc) & (o != k))(lambda: gp_rows.pass_on(k))
            pl.when(c != kc)(lambda: gp_rows.wait_mate(k))

    def multiply_back(z):
        size = 2 * og.rows
        start = pl.multiple_of(z * size, size)
        gp_ready(z)
        fetch = pltpu.make_async_copy(gp_panel.at[pl.ds(start, size)], gp_pair, load_sem.at[2])
        fetch.start()
        fetch.wait()

        @pl.loop(0, wi.shape[0] // COLS)
        def _(j):
            k = pl.ds(pl.multiple_of(j * COLS, COLS), COLS)
            product[pl.ds(start, size), k] = width_contract(gp_pair[...], wi[k, :]).astype(BF16)

    li.wait_own()
    load_wi.wait()
    at_step(0, multiply_back)
    steps = list(range(1, lines))
    early = steps[: max(1, 2 * len(steps) // 3)]
    li.step(1)
    at_step(lines - 2, finish)
    for s in early[1:]:
        li.step(s)
    at_step(lines - 1, finish)
    at_step(1, multiply_back)
    for s in steps[len(early):]:
        li.step(s)
    for s in steps[1:]:
        at_step(s, multiply_back)
    for k in order:
        first_copy(k).wait_send()
    gp_rows.wait_sends()

    store = pltpu.make_async_copy(product, out_panel, load_sem.at[2])
    store.start()

    for k in order[:-1]:
        second_copy(k).wait_send()
    act_rows.end()
    og.end()
    for s in range(lines):
        if s == 0:
            li.wait_mate(li.z)
        else:
            pl.when(li.z >= s)(lambda: li.wait_mate(li.z - s))
            pl.when(li.z + s < lines)(lambda: li.wait_mate(li.z + s))
    li.end()
    store.wait()


def hidden(n_row, n_col, layer_input, out_grad, preact, weight_in, weight_out):
    t, d = layer_input.shape
    rows, f = preact.shape
    tokens = t * n_col
    outer = n_row // 2
    any_spec = pl.BlockSpec(memory_space=pltpu.HBM)
    return pl.pallas_call(
        functools.partial(hidden_kernel, n_row, n_col),
        out_shape=[
            jax.ShapeDtypeStruct((tokens, d), BF16),
            jax.ShapeDtypeStruct((tokens, d), BF16),
            jax.ShapeDtypeStruct((tokens, f), BF16),
            jax.ShapeDtypeStruct((tokens, f), BF16),
            jax.ShapeDtypeStruct((tokens, d), BF16),
        ],
        in_specs=[any_spec] * 5,
        out_specs=[any_spec] * 5,
        scratch_shapes=[
            pltpu.VMEM((d, f), BF16),
            pltpu.VMEM((f, d), BF16),
            pltpu.VMEM((2 * t, d), BF16),
            pltpu.VMEM((2 * t, f), BF16),
            pltpu.VMEM((tokens, f), BF16),
            pltpu.VMEM((tokens, d), BF16),
            pltpu.VMEM((rows, f), BF16),
            pltpu.VMEM((rows, f), BF16),
            pltpu.VMEM((rows, f), F32),
            pltpu.VMEM((outer, rows, f), BF16),
            pltpu.VMEM((outer, rows, f), BF16),
            pltpu.VMEM((outer, rows, f), BF16),
            pltpu.VMEM((rows, f), BF16),
            pltpu.SemaphoreType.DMA((4,)),
        ]
        + [pltpu.SemaphoreType.DMA((outer,))] * 4
        + col_sems(n_col) * 2
        + row_sems(n_row) * 2,
        compiler_params=pltpu.CompilerParams(
            collective_id=0, has_side_effects=True, vmem_limit_bytes=58 * 2**20
        ),
        cost_estimate=pl.CostEstimate(
            flops=4 * tokens * d * f, bytes_accessed=4 * (f * d + 2 * tokens * (d + f)), transcendentals=rows * f
        ),
        name="hidden",
    )(layer_input, out_grad, preact, weight_in, weight_out)


def col_scatter(n_col, panel, others):
    lines = n_col // 2
    me = lax.axis_index("col")
    z, x = me // 2, me % 2
    rows = panel.shape[0] // n_col
    order = np.array([sorted(range(lines), key=lambda t: (-abs(t - p), t)) for p in range(lines)])
    place = np.argsort(order, axis=1)
    order, place = jnp.asarray(order, jnp.int32), jnp.asarray(place, jnp.int32)
    swap = [(i, i + 1 - 2 * (i % 2)) for i in range(n_col)]
    sums = []

    def of(target):
        at = place[z, jnp.clip(target, 0, lines - 1)]
        found = sums[0]
        for i in range(1, len(sums)):
            found = jnp.where(at == i, sums[i], found)
        return found.astype(F32)

    up = down = None
    for step in range(lines):
        at = order[z, step] * 2
        away = lax.dynamic_slice_in_dim(panel, (at + 1 - x) * rows, rows, 0)
        keep = lax.dynamic_slice_in_dim(panel, (at + x) * rows, rows, 0)
        if step in others:
            keep, others[step] = lax.optimization_barrier((keep, others[step]))
        got = lax.ppermute(away, "col", swap)
        sums.append((keep.astype(F32) + got.astype(F32)).astype(BF16))
        far = lines - 1 - step
        going_up, going_down = of(z + far), of(z - far)
        if step > 0:
            going_up, going_down = going_up + up.astype(F32), going_down + down.astype(F32)
        if far > 0:
            ups = [(2 * p + i, 2 * p + 2 + i) for p in range(step + 1) for i in range(2)]
            downs = [(n_col - 1 - a, n_col - 1 - b) for a, b in ups]
            up = lax.ppermute(going_up.astype(BF16), "col", ups)
            down = lax.ppermute(going_down.astype(BF16), "col", downs)
    return (going_up + down.astype(F32)).astype(BF16), others


def local(n_row, n_col, layer_input, out_grad, preact, weight_in, weight_out):
    li_panel, og_panel, act_panel, gp_panel, out_panel = hidden(
        n_row, n_col, layer_input, out_grad, preact, weight_in, weight_out
    )
    beside = {0: token_contract(act_panel, og_panel), 2: token_contract(li_panel, gp_panel)}
    input_grad, beside = col_scatter(n_col, out_panel, beside)
    return (input_grad, beside[2], beside[0])


def solution(mesh):
    placed = (P("col", "row"), P("col", "row"), P("row", "col"), P("row", "col"), P("col", "row"))
    return jax.shard_map(
        functools.partial(local, mesh.shape["row"], mesh.shape["col"]),
        mesh=mesh,
        in_specs=placed,
        out_specs=(P("col", "row"), P("row", "col"), P("col", "row")),
        check_vma=False,
    )
```
